32 devices in a mesh: groups: 2 (over x), tm: 16 (over z, y, core).
Axes of the slice: x: 2, y: 2, z: 4, core: 2. Of those that a mesh axis runs over, the one named last changes fastest.
Arguments:
- process_noise: bfloat16 [1024, 64, 1024], P(('groups', 'tm')), parts along dimension 0, may hold values from -6 to 6
- gauge_reads: bfloat16 [1024, 96, 1024], P(('groups', 'tm')), parts along dimension 0, may hold values from -6 to 6
- sensor_active: int32 [1024, 96], P(('groups', 'tm')), parts along dimension 0, may hold values 0 or 1
- sensor_link: int32 [96], replicated, may hold values from 0 to 31
- reflectors: float32 [8, 64], P('groups'), parts along dimension 0, may hold values from -6 to 6
- decay_rates: float32 [64], P('groups'), parts along dimension 0, may hold values from 9.765625e-05 to 0.04
- turn_angles: float32 [64], P('groups'), parts along dimension 0, may hold values from -3.140625 to 3.140625
- gauge_gain: float32 [128], P('groups'), parts along dimension 0, may hold values from 0.01 to 0.05
Outputs:
- smoothed: float32 [1024, 64, 1024], P(('groups', 'tm')), parts along dimension 0
The draws below stay inside these ranges and needn't reach their ends.
There are 2 independent parts, one for each index of `groups`. The reference program is written for one: setup_inputs(seed, part) draws one part's arguments, and reference() takes and returns one part's arrays. A program takes and returns all parts, laid end to end along the dimension named above; an argument that names none is the same for every part. Nothing has to cross between parts.
All inputs are finite; a program needn't handle non-finite values. No bound on the sum of `sensor_active` on one device may be relied on, other than what follows from the above.
Results may differ from the reference program's by a relative error of at most 0.0038.
Values sent between devices are 32-bit elements; how exact they have to be, the bound alone decides.
A program may use at most 128 MiB of HBM per device.

```python
import math
import jax
import jax.numpy as jnp
from jax import lax

S = 64
M = 96
REFLECTIONS = 4
RUNS = 1024
LINKS = 32
LENGTH = 512


def with_ends(result, rng, low, high):
    spot = [jax.random.randint(jax.random.fold_in(rng, axis), (), 0, length) for axis, length in enumerate(result.shape)]
    main_axis = result.shape.index(max(result.shape))
    next_to = spot[:main_axis] + [(spot[main_axis] + 1) % result.shape[main_axis]] + spot[main_axis + 1:]
    return result.at[tuple(spot)].set(low).at[tuple(next_to)].set(high)


def shard_levels(rng, extent, shards, least, largest):
    loudness, own = 1.0, jax.random.fold_in(rng, 6)
    for position, shards_of in shards:
        heights = jnp.exp(jax.random.uniform(jax.random.fold_in(own, position), (shards_of,), jnp.float32, least / len(shards), largest / len(shards)))
        loudness = loudness * jnp.repeat(heights, extent[position] // shards_of).reshape([-1 if axis == position else 1 for axis in range(len(extent))])
    return loudness


def scatter_about(stream_key, shape, scale, reach, cuts=(), held_as=jnp.bfloat16):
    entries = jax.random.normal(stream_key, shape, jnp.float32) * scale
    if len(cuts) > 0:
        entries = shard_levels(stream_key, shape, cuts, -0.22, 0.18) * entries
    return jnp.clip(entries, min=-reach, max=reach).astype(held_as)


def setup_inputs(seed: int = 0, part: int = 0) -> dict:
    seeds = jax.random.split(jax.random.key(seed), 9)
    part_splits = jax.random.split(jax.random.fold_in(seeds[8], part), 9)
    return {
        "process_noise": scatter_about(part_splits[0], (LENGTH, S, RUNS), 1.0, 6.0, ((0, 16),)),
        "gauge_reads": scatter_about(part_splits[1], (LENGTH, M, RUNS), 1.0, 6.0, ((0, 16),)),
        "sensor_active": with_ends((jax.random.randint(part_splits[2], (LENGTH, M), 0, 5) < 2).astype(jnp.int32), jax.random.fold_in(part_splits[2], 1), 0, 1),
        "sensor_link": with_ends(jax.random.randint(seeds[3], (M,), 0, LINKS), jax.random.fold_in(seeds[3], 1), 0, LINKS - 1).astype(jnp.int32),
        "reflectors": scatter_about(part_splits[4], (REFLECTIONS, S), 1.0, 6.0, (), jnp.float32),
        "decay_rates": jnp.clip(jnp.exp(jax.random.uniform(part_splits[5], (LINKS,), jnp.float32, math.log(9.765625145519152e-05), math.log(0.04))), 9.765625145519152e-05, 0.04),
        "turn_angles": jnp.clip(jax.random.uniform(part_splits[6], (LINKS,), jnp.float32, -3.140625, 3.140625), -3.140625, 3.140625),
        "gauge_gain": jnp.clip(jax.random.uniform(part_splits[7], (S,), jnp.float32, 0.01, 0.05), 0.01, 0.05),
    }


exact_mode = lax.Precision.HIGHEST

def rotation_basis(reflectors):
    width_all = reflectors.shape[1]
    rotation = jnp.eye(width_all, dtype=jnp.float32)
    for number in range(reflectors.shape[0]):
        vector = reflectors[number].astype(jnp.float32)
        factor = 2.0 / (jnp.sum(vector * vector) + 1e-06)
        rotation = rotation - factor * jnp.outer(jnp.dot(rotation, vector, precision=exact_mode), vector)
    return rotation

def pair_blocks(decay_rates, turn_angles):
    radius = jnp.exp(-decay_rates)
    cosine = jnp.repeat(radius * jnp.cos(turn_angles), 2)
    sine_part = jnp.repeat(radius * jnp.sin(turn_angles), 2)
    positions = jnp.arange(cosine.shape[0])
    pair_index = positions // 2
    parity = positions % 2
    same_pair = pair_index[:, None] == pair_index[None, :]
    same_parity = parity[:, None] == parity[None, :]
    upper = parity[:, None] == 0
    element = jnp.where(same_parity, cosine[:, None], jnp.where(upper, -sine_part[:, None], sine_part[:, None]))
    return jnp.where(same_pair, element, 0.0).astype(jnp.float32)

def model_terms(process_noise, gauge_reads, sensor_active, sensor_link, reflectors, decay_rates, turn_angles, gauge_gain):
    rotation = rotation_basis(reflectors)
    blocks = pair_blocks(decay_rates, turn_angles)
    transition = jnp.dot(jnp.dot(rotation, blocks, precision=exact_mode), rotation.T, precision=exact_mode)
    positions = jnp.arange(gauge_gain.shape[0]).astype(jnp.int32)
    onehot = (positions[None, :] == 2 * sensor_link[:, None]).astype(jnp.float32)
    active_float = sensor_active.astype(jnp.float32)
    counts = jnp.dot(active_float, onehot, precision=exact_mode)
    retain = jnp.exp(counts * jnp.log1p(-gauge_gain)[None, :])
    spread_scale = jnp.repeat(jnp.sqrt(-jnp.expm1(-2.0 * decay_rates)), 2)
    rotation_low = lax.optimization_barrier(rotation.astype(jnp.bfloat16)).astype(jnp.float32)
    scaled_noise = (spread_scale[None, :, None] * process_noise.astype(jnp.float32)).astype(jnp.bfloat16)
    scaled_noise = lax.optimization_barrier(scaled_noise).astype(jnp.float32)
    gauge_masked = active_float[:, :, None] * gauge_reads.astype(jnp.float32)
    noise_term = jnp.einsum('ij,tjr->tir', rotation_low, scaled_noise, precision=exact_mode)
    gauge_term = jnp.einsum('jk,tjr->tkr', onehot, gauge_masked, precision=exact_mode)
    offsets = noise_term + gauge_gain[None, :, None] * gauge_term
    return (transition, retain, offsets)

def reference(process_noise, gauge_reads, sensor_active, sensor_link, reflectors, decay_rates, turn_angles, gauge_gain):
    transition, retain, offsets = model_terms(process_noise, gauge_reads, sensor_active, sensor_link, reflectors, decay_rates, turn_angles, gauge_gain)

    def forward(estimate, inputs):
        keep_rate, offset = inputs
        estimate = keep_rate[:, None] * jnp.dot(transition, estimate, precision=exact_mode) + offset
        return (estimate, estimate)
    start = jnp.zeros(offsets.shape[1:], jnp.float32)
    _, filtered = lax.scan(forward, start, (retain, offsets))
    back_keep = retain.at[-1].set(0.0)
    predicted = jnp.einsum('ij,tjr->tir', transition, filtered, precision=exact_mode)
    pulled = jnp.einsum('ji,tjr->tir', transition, back_keep[:, :, None] * predicted, precision=exact_mode)
    corrections = filtered - pulled

    def backward(estimate, inputs):
        keep_rate, offset = inputs
        estimate = jnp.dot(transition.T, keep_rate[:, None] * estimate, precision=exact_mode) + offset
        return (estimate, estimate)
    _, smoothed = lax.scan(backward, start, (back_keep, corrections), reverse=True)
    return smoothed
```

```python
import jax
import jax.numpy as jnp
from jax import lax
from jax.experimental import pallas as pl
from jax.experimental.pallas import tpu as pltpu
from jax.sharding import PartitionSpec as P

exact_mode = lax.Precision.HIGHEST
bf16 = jnp.bfloat16
f32 = jnp.float32


def rotation_basis(reflectors):
    width_all = reflectors.shape[1]
    rotation = jnp.eye(width_all, dtype=f32)
    for number in range(reflectors.shape[0]):
        vector = reflectors[number]
        factor = 2.0 / (jnp.sum(vector * vector) + 1e-06)
        rotation = rotation - factor * jnp.outer(
            jnp.dot(rotation, vector, precision=exact_mode), vector
        )
    return rotation


def pair_blocks(decay_rates, turn_angles):
    radius = jnp.exp(-decay_rates)
    cosine = jnp.repeat(radius * jnp.cos(turn_angles), 2)
    sine_part = jnp.repeat(radius * jnp.sin(turn_angles), 2)
    positions = jnp.arange(cosine.shape[0])
    pair_index = positions // 2
    parity = positions % 2
    same_pair = pair_index[:, None] == pair_index[None, :]
    same_parity = parity[:, None] == parity[None, :]
    upper = parity[:, None] == 0
    element = jnp.where(
        same_parity, cosine[:, None], jnp.where(upper, -sine_part[:, None], sine_part[:, None])
    )
    return jnp.where(same_pair, element, 0.0)


def two_parts(x):
    high = lax.reduce_precision(x, 8, 7)
    return high.astype(bf16), (x - high).astype(bf16)


def map_parts(matrix):
    high, low = two_parts(matrix)
    return jnp.concatenate([high, low, high], axis=1)


def state_parts(x):
    high = x.astype(bf16)
    low = (x - high.astype(f32)).astype(bf16)
    return jnp.concatenate([high, high, low], axis=0)


def dot32(a, b):
    return jnp.dot(a, b, preferred_element_type=f32)


def local_kernel(
    blocks, per, noise, gauges, weights, spread, retain, keep, fwd_map, bwd_map, trans,
    partial, maps, end_state, end_map, first_state, first_map,
    filt, filt_x, pred, pred_x, run, run_x,
):
    step = pl.program_id(0)
    width = trans.shape[0]

    @pl.when(step == 0)
    def _():
        run[...] = jnp.zeros_like(run)
        run_x[...] = jnp.concatenate([trans[...], jnp.zeros_like(trans)], axis=1)

    @pl.when(step < blocks)
    def _():
        p, px = run[...], run_x[...]
        for i in range(per):
            t = step * per + i
            scaled = (spread[...] * noise[i].astype(f32)).astype(bf16)
            reads = gauges[i]
            offset = dot32(weights[i], jnp.concatenate([scaled, reads, reads], axis=0))
            rate = retain[t]
            f = rate * p + offset
            fx = rate * px
            filt[t] = f
            filt_x[t] = fx
            p = dot32(fwd_map[...], state_parts(f))
            px = dot32(fwd_map[...], state_parts(fx))
            pred[t] = p
            pred_x[t] = px
        run[...] = p
        run_x[...] = px

        @pl.when(step == blocks - 1)
        def _():
            end_state[...] = f
            end_map[...] = fx
            run[...] = jnp.zeros_like(run)
            row = lax.broadcasted_iota(jnp.int32, run_x.shape, 0)
            col = lax.broadcasted_iota(jnp.int32, run_x.shape, 1)
            run_x[...] = jnp.where(col == row + width, 1.0, 0.0)

    @pl.when(step >= blocks)
    def _():
        s, sx = run[...], run_x[...]
        for i in reversed(range(per)):
            t = (2 * blocks - 1 - step) * per + i
            rate = keep[t]
            s = filt[t] + dot32(bwd_map[...], state_parts(rate * (s - pred[t])))
            sx = filt_x[t] + dot32(bwd_map[...], state_parts(rate * (sx - pred_x[t])))
            partial[i] = s
            maps[i] = sx
        run[...] = s
        run_x[...] = sx

        @pl.when(step == 2 * blocks - 1)
        def _():
            first_state[...] = s
            first_map[...] = sx


def local_pass(noise, gauges, weights, spread, retain, keep, fwd_map, bwd_map, trans):
    steps, width, runs = noise.shape
    per = 4
    blocks = steps // per
    ahead = lambda i: (jnp.minimum(i, blocks - 1), 0, 0)
    back = lambda i: (jnp.minimum(2 * blocks - 1 - i, blocks - 1), 0, 0)
    whole2 = lambda i: (0, 0)
    whole3 = lambda i: (0, 0, 0)
    full = lambda x: pl.BlockSpec(x.shape, whole3 if x.ndim == 3 else whole2)
    extra = 2 * width
    body = lambda *refs: local_kernel(blocks, per, *refs)
    return pl.pallas_call(
        body,
        grid=(2 * blocks,),
        in_specs=[
            pl.BlockSpec((per,) + noise.shape[1:], ahead),
            pl.BlockSpec((per,) + gauges.shape[1:], ahead),
            pl.BlockSpec((per,) + weights.shape[1:], ahead),
            full(spread), full(retain), full(keep), full(fwd_map), full(bwd_map), full(trans),
        ],
        out_specs=[
            pl.BlockSpec((per, width, runs), back),
            pl.BlockSpec((per, width, extra), back),
            pl.BlockSpec((width, runs), whole2),
            pl.BlockSpec((width, extra), whole2),
            pl.BlockSpec((width, runs), whole2),
            pl.BlockSpec((width, extra), whole2),
        ],
        out_shape=[
            jax.ShapeDtypeStruct((steps, width, runs), f32),
            jax.ShapeDtypeStruct((steps, width, extra), f32),
            jax.ShapeDtypeStruct((width, runs), f32),
            jax.ShapeDtypeStruct((width, extra), f32),
            jax.ShapeDtypeStruct((width, runs), f32),
            jax.ShapeDtypeStruct((width, extra), f32),
        ],
        scratch_shapes=[
            pltpu.VMEM((steps, width, runs), f32),
            pltpu.VMEM((steps, width, extra), f32),
            pltpu.VMEM((steps, width, runs), f32),
            pltpu.VMEM((steps, width, extra), f32),
            pltpu.VMEM((width, runs), f32),
            pltpu.VMEM((width, extra), f32),
        ],
        compiler_params=pltpu.CompilerParams(vmem_limit_bytes=52 * 2**20),
    )(noise, gauges, weights, spread, retain, keep, fwd_map, bwd_map, trans)


def split_dot(matrix, state):
    high = matrix.astype(bf16)
    low = (matrix - high.astype(f32)).astype(bf16)
    return dot32(jnp.concatenate([high, low, high], axis=1), state_parts(state))


def border_kernel(states, maps, carries):
    count, double, runs = states.shape
    width = double // 2
    carry = jnp.zeros((width, runs), f32)
    for d in range(count):
        carries[d, :width] = carry
        if d < count - 1:
            carry = states[d, :width] + split_dot(maps[d, :, : 2 * width], jnp.concatenate([carry, jnp.zeros_like(carry)], axis=0))
    carry = jnp.zeros((width, runs), f32)
    for d in reversed(range(count)):
        carries[d, width:] = carry
        if d > 0:
            carry = states[d, width:] + split_dot(
                maps[d, :, 2 * width :], jnp.concatenate([carries[d, :width], carry], axis=0)
            )


def border_pass(states, maps):
    return pl.pallas_call(
        border_kernel,
        out_shape=jax.ShapeDtypeStruct(states.shape, f32),
        compiler_params=pltpu.CompilerParams(vmem_limit_bytes=32 * 2**20),
    )(states, maps)


def close_kernel(per, partial, maps, carries, smoothed, parts):
    @pl.when(pl.program_id(0) == 0)
    def _():
        parts[...] = state_parts(carries[...])

    for i in range(per):
        m = maps[i]
        high = m.astype(bf16)
        low = (m - high.astype(f32)).astype(bf16)
        smoothed[i] = partial[i] + dot32(jnp.concatenate([high, low, high], axis=1), parts[...])


def close_pass(partial, maps, carries):
    steps, width, runs = partial.shape
    per = 4
    body = lambda *refs: close_kernel(per, *refs)
    along = lambda i: (i, 0, 0)
    return pl.pallas_call(
        body,
        grid=(steps // per,),
        in_specs=[
            pl.BlockSpec((per, width, runs), along),
            pl.BlockSpec((per,) + maps.shape[1:], along),
            pl.BlockSpec(carries.shape, lambda i: (0, 0)),
        ],
        out_specs=pl.BlockSpec((per, width, runs), along),
        out_shape=jax.ShapeDtypeStruct(partial.shape, f32),
        scratch_shapes=[pltpu.VMEM((3 * carries.shape[0], runs), bf16)],
        compiler_params=pltpu.CompilerParams(vmem_limit_bytes=32 * 2**20),
    )(partial, maps, carries)


def shards(
    process_noise,
    gauge_reads,
    sensor_active,
    sensor_link,
    reflectors,
    decay_rates,
    turn_angles,
    gauge_gain,
):
    steps, width, runs = process_noise.shape
    count = lax.axis_size("tm")
    rotation = rotation_basis(reflectors)
    blocks = pair_blocks(decay_rates, turn_angles)
    transition = jnp.dot(
        jnp.dot(rotation, blocks, precision=exact_mode), rotation.T, precision=exact_mode
    )
    positions = jnp.arange(width)
    onehot = (positions[None, :] == 2 * sensor_link[:, None]).astype(f32)
    active = sensor_active.astype(f32)
    counts = jnp.dot(active, onehot, precision=exact_mode)
    retain = jnp.exp(counts * jnp.log1p(-gauge_gain)[None, :])
    spread = jnp.repeat(jnp.sqrt(-jnp.expm1(-2.0 * decay_rates)), 2)
    last_row = (jnp.arange(steps) == steps - 1)[:, None]
    final_device = lax.axis_index("tm") == count - 1
    keep = jnp.where(jnp.logical_and(last_row, final_device), 0.0, retain)
    gain_high, gain_low = two_parts(gauge_gain)
    placed = (onehot.T.astype(bf16))[None] * sensor_active.astype(bf16)[:, None, :]
    weights = jnp.concatenate(
        [
            jnp.broadcast_to(rotation.astype(bf16)[None], (steps, width, width)),
            gain_high[None, :, None] * placed,
            gain_low[None, :, None] * placed,
        ],
        axis=2,
    )
    partial, maps, end_state, end_map, first_state, first_map = local_pass(
        process_noise, gauge_reads, weights, spread[:, None], retain[:, :, None],
        keep[:, :, None], map_parts(transition), map_parts(transition.T), transition,
    )
    own = jnp.concatenate([end_state, first_state], axis=0)
    own = own.reshape(2 * width, count, runs // count).transpose(1, 0, 2)
    states = lax.all_to_all(own, "tm", 0, 0)
    all_maps = lax.all_gather(jnp.concatenate([end_map, first_map], axis=1), "tm")
    carries = border_pass(states, all_maps)
    carries = lax.all_to_all(carries, "tm", 0, 0)
    carries = carries.transpose(1, 0, 2).reshape(2 * width, runs)
    return close_pass(partial, maps, carries)


def solution(mesh):
    in_specs = (
        P(("groups", "tm"), None, None),
        P(("groups", "tm"), None, None),
        P(("groups", "tm"), None),
        P(),
        P("groups", None),
        P("groups"),
        P("groups"),
        P("groups"),
    )
    out_specs = P(("groups", "tm"), None, None)
    return jax.shard_map(shards, mesh=mesh, in_specs=in_specs, out_specs=out_specs, check_vma=False)
```

```python
import jax
import jax.numpy as jnp
from jax import lax
from jax.experimental import pallas as pl
from jax.experimental.pallas import tpu as pltpu
from jax.sharding import PartitionSpec as P

exact_mode = lax.Precision.HIGHEST
bf16 = jnp.bfloat16
f32 = jnp.float32


def rotation_basis(reflectors):
    width_all = reflectors.shape[1]
    rotation = jnp.eye(width_all, dtype=f32)
    for number in range(reflectors.shape[0]):
        vector = reflectors[number]
        factor = 2.0 / (jnp.sum(vector * vector) + 1e-06)
        rotation = rotation - factor * jnp.outer(
            jnp.dot(rotation, vector, precision=exact_mode), vector
        )
    return rotation


def pair_blocks(decay_rates, turn_angles):
    radius = jnp.exp(-decay_rates)
    cosine = jnp.repeat(radius * jnp.cos(turn_angles), 2)
    sine_part = jnp.repeat(radius * jnp.sin(turn_angles), 2)
    positions = jnp.arange(cosine.shape[0])
    pair_index = positions // 2
    parity = positions % 2
    same_pair = pair_index[:, None] == pair_index[None, :]
    same_parity = parity[:, None] == parity[None, :]
    upper = parity[:, None] == 0
    element = jnp.where(
        same_parity, cosine[:, None], jnp.where(upper, -sine_part[:, None], sine_part[:, None])
    )
    return jnp.where(same_pair, element, 0.0)


def two_parts(x):
    high = lax.reduce_precision(x, 8, 7)
    return high.astype(bf16), (x - high).astype(bf16)


def map_parts(matrix):
    high, low = two_parts(matrix)
    return jnp.concatenate([high, low, high], axis=1)


def state_parts(x):
    high = x.astype(bf16)
    low = (x - high.astype(f32)).astype(bf16)
    return jnp.concatenate([high, high, low], axis=0)


def dot32(a, b):
    return jnp.dot(a, b, preferred_element_type=f32)


def local_kernel(
    blocks, per, noise, gauges, weights, spread, retain, keep, fwd_map, bwd_map, trans,
    partial, maps, end_state, end_map, first_state, first_map,
    filt, filt_x, pred, pred_x, run, run_x,
):
    step = pl.program_id(0)
    width = trans.shape[0]

    @pl.when(step == 0)
    def _():
        run[...] = jnp.zeros_like(run)
        run_x[...] = jnp.concatenate([trans[...], jnp.zeros_like(trans)], axis=1)

    @pl.when(step < blocks)
    def _():
        p, px = run[...], run_x[...]
        for i in range(per):
            t = step * per + i
            scaled = (spread[...] * noise[i].astype(f32)).astype(bf16)
            reads = gauges[i]
            offset = dot32(weights[i], jnp.concatenate([scaled, reads, reads], axis=0))
            rate = retain[t]
            f = rate * p + offset
            fx = rate * px
            filt[t] = f
            filt_x[t] = fx
            p = dot32(fwd_map[...], state_parts(f))
            px = dot32(fwd_map[...], state_parts(fx))
            pred[t] = p
            pred_x[t] = px
        run[...] = p
        run_x[...] = px

        @pl.when(step == blocks - 1)
        def _():
            end_state[...] = f
            end_map[...] = fx
            run[...] = jnp.zeros_like(run)
            row = lax.broadcasted_iota(jnp.int32, run_x.shape, 0)
            col = lax.broadcasted_iota(jnp.int32, run_x.shape, 1)
            run_x[...] = jnp.where(col == row + width, 1.0, 0.0)

    @pl.when(step >= blocks)
    def _():
        s, sx = run[...], run_x[...]
        for i in reversed(range(per)):
            t = (2 * blocks - 1 - step) * per + i
            rate = keep[t]
            s = filt[t] + dot32(bwd_map[...], state_parts(rate * (s - pred[t])))
            sx = filt_x[t] + dot32(bwd_map[...], state_parts(rate * (sx - pred_x[t])))
            partial[i] = s
            maps[i] = sx
        run[...] = s
        run_x[...] = sx

        @pl.when(step == 2 * blocks - 1)
        def _():
            first_state[...] = s
            first_map[...] = sx


def local_pass(noise, gauges, weights, spread, retain, keep, fwd_map, bwd_map, trans):
    steps, width, runs = noise.shape
    per = 4
    blocks = steps // per
    ahead = lambda i: (jnp.minimum(i, blocks - 1), 0, 0)
    back = lambda i: (jnp.minimum(2 * blocks - 1 - i, blocks - 1), 0, 0)
    whole2 = lambda i: (0, 0)
    whole3 = lambda i: (0, 0, 0)
    full = lambda x: pl.BlockSpec(x.shape, whole3 if x.ndim == 3 else whole2)
    extra = 2 * width
    body = lambda *refs: local_kernel(blocks, per, *refs)
    return pl.pallas_call(
        body,
        grid=(2 * blocks,),
        in_specs=[
            pl.BlockSpec((per,) + noise.shape[1:], ahead),
            pl.BlockSpec((per,) + gauges.shape[1:], ahead),
            pl.BlockSpec((per,) + weights.shape[1:], ahead),
            full(spread), full(retain), full(keep), full(fwd_map), full(bwd_map), full(trans),
        ],
        out_specs=[
            pl.BlockSpec((per, width, runs), back),
            pl.BlockSpec((per, width, extra), back),
            pl.BlockSpec((width, runs), whole2),
            pl.BlockSpec((width, extra), whole2),
            pl.BlockSpec((width, runs), whole2),
            pl.BlockSpec((width, extra), whole2),
        ],
        out_shape=[
            jax.ShapeDtypeStruct((steps, width, runs), f32),
            jax.ShapeDtypeStruct((steps, width, extra), f32),
            jax.ShapeDtypeStruct((width, runs), f32),
            jax.ShapeDtypeStruct((width, extra), f32),
            jax.ShapeDtypeStruct((width, runs), f32),
            jax.ShapeDtypeStruct((width, extra), f32),
        ],
        scratch_shapes=[
            pltpu.VMEM((steps, width, runs), f32),
            pltpu.VMEM((steps, width, extra), f32),
            pltpu.VMEM((steps, width, runs), f32),
            pltpu.VMEM((steps, width, extra), f32),
            pltpu.VMEM((width, runs), f32),
            pltpu.VMEM((width, extra), f32),
        ],
        compiler_params=pltpu.CompilerParams(vmem_limit_bytes=52 * 2**20),
    )(noise, gauges, weights, spread, retain, keep, fwd_map, bwd_map, trans)


def split_dot(matrix, state):
    high = matrix.astype(bf16)
    low = (matrix - high.astype(f32)).astype(bf16)
    return dot32(jnp.concatenate([high, low, high], axis=1), state_parts(state))


def border_kernel(
    count, group, own, own_map, result, states, maps, carries, landed,
    state_send, state_recv, far_send, far_recv, near_send, near_recv, back_send, back_recv,
):
    me = lax.axis_index("tm")
    width, double = own.shape[1:]
    runs = double // 2
    far = count // group
    place, seat = lax.div(me, group), lax.rem(me, group)

    def push(source, target, send, recv, where):
        copy = pltpu.make_async_remote_copy(
            src_ref=source, dst_ref=target, send_sem=send, recv_sem=recv,
            device_id={"tm": where}, device_id_type=pl.DeviceIdType.MESH,
        )
        copy.start()
        return copy

    barrier = pltpu.get_barrier_semaphore()
    for k in range(1, count):
        pl.semaphore_signal(
            barrier, inc=1, device_id={"tm": lax.rem(me + k, count)},
            device_id_type=pl.DeviceIdType.MESH,
        )
    pl.semaphore_wait(barrier, count - 1)

    far_copies = [
        push(own_map, maps.at[seat, place], far_send.at[k], far_recv.at[k],
             lax.rem(place + k, far) * group + seat)
        for k in range(1, far)
    ]
    copies = [
        push(own.at[lax.rem(me + k, count)], states.at[me], state_send.at[k], state_recv.at[k],
             lax.rem(me + k, count))
        for k in range(1, count)
    ]
    states[me] = own[me]
    maps[seat, place] = own_map[...]
    for copy in far_copies:
        copy.wait()
    copies += [
        push(maps.at[seat], maps.at[seat], near_send.at[k], near_recv.at[k],
             place * group + lax.rem(seat + k, group))
        for k in range(1, group)
    ]
    for copy in copies:
        copy.wait()

    carry = jnp.zeros((width, runs), f32)
    ahead, pulled = [], []
    for d in range(count):
        both = maps[d % group, d // group]
        stay, turn = both[:, :width], both[:, width:]
        ahead.append(carry)
        pulled.append(states[d, :, runs:] + split_dot(turn, carry))
        if d < count - 1:
            carry = states[d, :, :runs] + split_dot(stay, carry)
    carry = jnp.zeros((width, runs), f32)
    for d in reversed(range(count)):
        carries[d] = jnp.concatenate([ahead[d], carry], axis=1)
        if d > 0:
            stay = maps[d % group, d // group][:, :width]
            carry = pulled[d] + split_dot(stay.T, carry)

    copies = [
        push(carries.at[lax.rem(me + k, count)], landed.at[me], back_send.at[k], back_recv.at[k],
             lax.rem(me + k, count))
        for k in range(1, count)
    ]
    landed[me] = carries[me]
    for copy in copies:
        copy.wait()
    result[...] = landed[...]


def border_pass(own, own_map):
    count = own.shape[0]
    group = 4 if count % 4 == 0 else 1
    far = count // group
    dma = pltpu.SemaphoreType.DMA
    return pl.pallas_call(
        lambda *refs: border_kernel(count, group, *refs),
        in_specs=[pl.BlockSpec(memory_space=pltpu.VMEM)] * 2,
        out_specs=pl.BlockSpec(memory_space=pltpu.VMEM),
        out_shape=jax.ShapeDtypeStruct(own.shape, f32),
        scratch_shapes=[
            pltpu.VMEM(own.shape, f32),
            pltpu.VMEM((group, far) + own_map.shape, f32),
            pltpu.VMEM(own.shape, f32),
            pltpu.VMEM(own.shape, f32),
            dma((count,)), dma((count,)), dma((far,)), dma((far,)),
            dma((group,)), dma((group,)), dma((count,)), dma((count,)),
        ],
        compiler_params=pltpu.CompilerParams(
            collective_id=0, has_side_effects=True, vmem_limit_bytes=32 * 2**20
        ),
    )(own, own_map)


def close_kernel(per, partial, maps, carries, smoothed, parts):
    @pl.when(pl.program_id(0) == 0)
    def _():
        parts[...] = state_parts(carries[...])

    for i in range(per):
        m = maps[i]
        high = m.astype(bf16)
        low = (m - high.astype(f32)).astype(bf16)
        smoothed[i] = partial[i] + dot32(jnp.concatenate([high, low, high], axis=1), parts[...])


def close_pass(partial, maps, carries):
    steps, width, runs = partial.shape
    per = 4
    body = lambda *refs: close_kernel(per, *refs)
    along = lambda i: (i, 0, 0)
    return pl.pallas_call(
        body,
        grid=(steps // per,),
        in_specs=[
            pl.BlockSpec((per, width, runs), along),
            pl.BlockSpec((per,) + maps.shape[1:], along),
            pl.BlockSpec(carries.shape, lambda i: (0, 0)),
        ],
        out_specs=pl.BlockSpec((per, width, runs), along),
        out_shape=jax.ShapeDtypeStruct(partial.shape, f32),
        scratch_shapes=[pltpu.VMEM((3 * carries.shape[0], runs), bf16)],
        compiler_params=pltpu.CompilerParams(vmem_limit_bytes=32 * 2**20),
    )(partial, maps, carries)


def shards(
    process_noise,
    gauge_reads,
    sensor_active,
    sensor_link,
    reflectors,
    decay_rates,
    turn_angles,
    gauge_gain,
):
    steps, width, runs = process_noise.shape
    count = lax.axis_size("tm")
    rotation = rotation_basis(reflectors)
    blocks = pair_blocks(decay_rates, turn_angles)
    transition = jnp.dot(
        jnp.dot(rotation, blocks, precision=exact_mode), rotation.T, precision=exact_mode
    )
    positions = jnp.arange(width)
    onehot = (positions[None, :] == 2 * sensor_link[:, None]).astype(f32)
    active = sensor_active.astype(f32)
    counts = jnp.dot(active, onehot, precision=exact_mode)
    retain = jnp.exp(counts * jnp.log1p(-gauge_gain)[None, :])
    spread = jnp.repeat(jnp.sqrt(-jnp.expm1(-2.0 * decay_rates)), 2)
    last_row = (jnp.arange(steps) == steps - 1)[:, None]
    final_device = lax.axis_index("tm") == count - 1
    keep = jnp.where(jnp.logical_and(last_row, final_device), 0.0, retain)
    gain_high, gain_low = two_parts(gauge_gain)
    placed = (onehot.T.astype(bf16))[None] * sensor_active.astype(bf16)[:, None, :]
    weights = jnp.concatenate(
        [
            jnp.broadcast_to(rotation.astype(bf16)[None], (steps, width, width)),
            gain_high[None, :, None] * placed,
            gain_low[None, :, None] * placed,
        ],
        axis=2,
    )
    partial, maps, end_state, end_map, first_state, first_map = local_pass(
        process_noise, gauge_reads, weights, spread[:, None], retain[:, :, None],
        keep[:, :, None], map_parts(transition), map_parts(transition.T), transition,
    )
    sliced = lambda x: x.reshape(width, count, runs // count).transpose(1, 0, 2)
    own = jnp.concatenate([sliced(end_state), sliced(first_state)], axis=2)
    own_map = jnp.concatenate([end_map[:, :width], first_map[:, :width]], axis=1)
    carries = border_pass(own, own_map)
    carries = carries.reshape(count, width, 2, runs // count).transpose(2, 1, 0, 3)
    carries = carries.reshape(2 * width, runs)
    return close_pass(partial, maps, carries)


def solution(mesh):
    in_specs = (
        P(("groups", "tm"), None, None),
        P(("groups", "tm"), None, None),
        P(("groups", "tm"), None),
        P(),
        P("groups", None),
        P("groups"),
        P("groups"),
        P("groups"),
    )
    out_specs = P(("groups", "tm"), None, None)
    return jax.shard_map(shards, mesh=mesh, in_specs=in_specs, out_specs=out_specs, check_vma=False)
```

```python
import jax
import jax.numpy as jnp
from jax import lax
from jax.experimental import pallas as pl
from jax.experimental.pallas import tpu as pltpu
from jax.sharding import PartitionSpec as P

exact_mode = lax.Precision.HIGHEST
bf16 = jnp.bfloat16
f32 = jnp.float32


def rotation_basis(reflectors):
    width_all = reflectors.shape[1]
    rotation = jnp.eye(width_all, dtype=f32)
    for number in range(reflectors.shape[0]):
        vector = reflectors[number]
        factor = 2.0 / (jnp.sum(vector * vector) + 1e-06)
        rotation = rotation - factor * jnp.outer(
            jnp.dot(rotation, vector, precision=exact_mode), vector
        )
    return rotation


def pair_blocks(decay_rates, turn_angles):
    radius = jnp.exp(-decay_rates)
    cosine = jnp.repeat(radius * jnp.cos(turn_angles), 2)
    sine_part = jnp.repeat(radius * jnp.sin(turn_angles), 2)
    positions = jnp.arange(cosine.shape[0])
    pair_index = positions // 2
    parity = positions % 2
    same_pair = pair_index[:, None] == pair_index[None, :]
    same_parity = parity[:, None] == parity[None, :]
    upper = parity[:, None] == 0
    element = jnp.where(
        same_parity, cosine[:, None], jnp.where(upper, -sine_part[:, None], sine_part[:, None])
    )
    return jnp.where(same_pair, element, 0.0)


def two_parts(x):
    high = lax.reduce_precision(x, 8, 7)
    return high.astype(bf16), (x - high).astype(bf16)


def map_parts(matrix):
    high, low = two_parts(matrix)
    return jnp.concatenate([high, low, high], axis=1)


def state_parts(x):
    high = x.astype(bf16)
    low = (x - high.astype(f32)).astype(bf16)
    return jnp.concatenate([high, high, low], axis=0)


def dot32(a, b):
    return jnp.dot(a, b, preferred_element_type=f32)


def local_kernel(
    blocks, per, noise, gauges, weights, spread, retain, keep, fwd_map, bwd_map, trans,
    partial, maps, end_state, end_map, first_state, first_map,
    filt, filt_x, pred, pred_x, run, run_x,
):
    step = pl.program_id(0)
    width = trans.shape[0]

    @pl.when(step == 0)
    def _():
        run[...] = jnp.zeros_like(run)
        run_x[...] = jnp.concatenate([trans[...], jnp.zeros_like(trans)], axis=1)

    @pl.when(step < blocks)
    def _():
        p, px = run[...], run_x[...]
        for i in range(per):
            t = step * per + i
            scaled = (spread[...] * noise[i].astype(f32)).astype(bf16)
            reads = gauges[i]
            offset = dot32(weights[i], jnp.concatenate([scaled, reads, reads], axis=0))
            rate = retain[t]
            f = rate * p + offset
            fx = rate * px
            filt[t] = f
            filt_x[t] = fx
            p = dot32(fwd_map[...], state_parts(f))
            px = dot32(fwd_map[...], state_parts(fx))
            pred[t] = p
            pred_x[t] = px
        run[...] = p
        run_x[...] = px

        @pl.when(step == blocks - 1)
        def _():
            end_state[...] = f
            end_map[...] = fx
            run[...] = jnp.zeros_like(run)
            row = lax.broadcasted_iota(jnp.int32, run_x.shape, 0)
            col = lax.broadcasted_iota(jnp.int32, run_x.shape, 1)
            run_x[...] = jnp.where(col == row + width, 1.0, 0.0)

    @pl.when(step >= blocks)
    def _():
        s, sx = run[...], run_x[...]
        for i in reversed(range(per)):
            t = (2 * blocks - 1 - step) * per + i
            rate = keep[t]
            s = filt[t] + dot32(bwd_map[...], state_parts(rate * (s - pred[t])))
            sx = filt_x[t] + dot32(bwd_map[...], state_parts(rate * (sx - pred_x[t])))
            partial[i] = s
            maps[i] = sx
        run[...] = s
        run_x[...] = sx

        @pl.when(step == 2 * blocks - 1)
        def _():
            first_state[...] = s
            first_map[...] = sx


def local_pass(noise, gauges, weights, spread, retain, keep, fwd_map, bwd_map, trans):
    steps, width, runs = noise.shape
    per = 4
    blocks = steps // per
    ahead = lambda i: (jnp.minimum(i, blocks - 1), 0, 0)
    back = lambda i: (jnp.minimum(2 * blocks - 1 - i, blocks - 1), 0, 0)
    whole2 = lambda i: (0, 0)
    whole3 = lambda i: (0, 0, 0)
    full = lambda x: pl.BlockSpec(x.shape, whole3 if x.ndim == 3 else whole2)
    extra = 2 * width
    body = lambda *refs: local_kernel(blocks, per, *refs)
    return pl.pallas_call(
        body,
        grid=(2 * blocks,),
        in_specs=[
            pl.BlockSpec((per,) + noise.shape[1:], ahead),
            pl.BlockSpec((per,) + gauges.shape[1:], ahead),
            pl.BlockSpec((per,) + weights.shape[1:], ahead),
            full(spread), full(retain), full(keep), full(fwd_map), full(bwd_map), full(trans),
        ],
        out_specs=[
            pl.BlockSpec((per, width, runs), back),
            pl.BlockSpec((per, width, extra), back),
            pl.BlockSpec((width, runs), whole2),
            pl.BlockSpec((width, extra), whole2),
            pl.BlockSpec((width, runs), whole2),
            pl.BlockSpec((width, extra), whole2),
        ],
        out_shape=[
            jax.ShapeDtypeStruct((steps, width, runs), f32),
            jax.ShapeDtypeStruct((steps, width, extra), f32),
            jax.ShapeDtypeStruct((width, runs), f32),
            jax.ShapeDtypeStruct((width, extra), f32),
            jax.ShapeDtypeStruct((width, runs), f32),
            jax.ShapeDtypeStruct((width, extra), f32),
        ],
        scratch_shapes=[
            pltpu.VMEM((steps, width, runs), f32),
            pltpu.VMEM((steps, width, extra), f32),
            pltpu.VMEM((steps, width, runs), f32),
            pltpu.VMEM((steps, width, extra), f32),
            pltpu.VMEM((width, runs), f32),
            pltpu.VMEM((width, extra), f32),
        ],
        compiler_params=pltpu.CompilerParams(vmem_limit_bytes=52 * 2**20),
    )(noise, gauges, weights, spread, retain, keep, fwd_map, bwd_map, trans)


def split_dot(matrix, state):
    high = matrix.astype(bf16)
    low = (matrix - high.astype(f32)).astype(bf16)
    return dot32(jnp.concatenate([high, low, high], axis=1), state_parts(state))


def border_kernel(sizes, end_state, first_state, end_map, first_map, result, *scratch):
    me = lax.axis_index("tm")
    width = end_state.shape[0]
    last = len(sizes) - 1
    strides, seats = [], []
    stride = 1
    for size in sizes:
        strides.append(stride)
        seats.append(lax.rem(lax.div(me, stride), size))
        stride *= size

    def peer(level, k):
        seat = seats[level]
        return me + (lax.rem(seat + k, sizes[level]) - seat) * strides[level]

    barrier = pltpu.get_barrier_semaphore()
    for level, size in enumerate(sizes):
        for k in range(1, size):
            pl.semaphore_signal(
                barrier, inc=1, device_id={"tm": peer(level, k)},
                device_id_type=pl.DeviceIdType.MESH,
            )
    pl.semaphore_wait(barrier, sum(sizes) - len(sizes))

    def push(source, target, send, recv, where):
        copy = pltpu.make_async_remote_copy(
            src_ref=source, dst_ref=target, send_sem=send, recv_sem=recv,
            device_id={"tm": where}, device_id_type=pl.DeviceIdType.MESH,
        )
        copy.start()
        return copy

    def solve(level, state, first, stay, turn):
        own, got, maps, back, landed, *sems = scratch[11 * level : 11 * (level + 1)]
        size, seat = sizes[level], seats[level]
        runs = state.shape[1] // size
        top = level == last
        maps[seat] = jnp.concatenate([stay, turn], axis=1)
        for j in range(size):
            part = slice(j * runs, (j + 1) * runs)
            own[j] = jnp.concatenate([state[:, part], first[:, part]], axis=1)
        copies = []
        for k in range(1, size):
            where = peer(level, k)
            copies.append(push(maps.at[seat], maps.at[seat], sems[0].at[k], sems[1].at[k], where))
            copies.append(
                push(own.at[lax.rem(seat + k, size)], got.at[seat], sems[2].at[k], sems[3].at[k], where)
            )
        got[seat] = own[seat]
        for copy in copies:
            copy.wait()

        row = lax.broadcasted_iota(jnp.int32, (width, 2 * width), 0)
        col = lax.broadcasted_iota(jnp.int32, (width, 2 * width), 1)
        zero = jnp.zeros((width, runs), f32)
        blank = jnp.zeros((width, 2 * width), f32)

        def wide(value, extra):
            return value if top else jnp.concatenate([value, extra], axis=1)

        ahead, pulled, behind = [], [], [None] * size
        carry = wide(zero, jnp.where(row == col, 1.0, 0.0))
        for d in range(size):
            tile, both = got[d], maps[d]
            ahead.append(carry)
            pulled.append(wide(tile[:, runs:], blank) + split_dot(both[:, width:], carry))
            if not (top and d == size - 1):
                carry = wide(tile[:, :runs], blank) + split_dot(both[:, :width], carry)
        end = carry
        carry = wide(zero, jnp.where(row + width == col, 1.0, 0.0))
        for d in reversed(range(size)):
            behind[d] = carry
            if not (top and d == 0):
                carry = pulled[d] + split_dot(maps[d][:, :width].T, carry)
        if not top:
            inner = slice(runs, runs + width)
            outer = jnp.concatenate(
                solve(level + 1, end[:, :runs], carry[:, :runs], end[:, inner], carry[:, inner]),
                axis=0,
            )
        for d in range(size):
            f, s = ahead[d], behind[d]
            if not top:
                f = f[:, :runs] + split_dot(f[:, runs:], outer)
                s = s[:, :runs] + split_dot(s[:, runs:], outer)
            back[d] = jnp.concatenate([f, s], axis=1)
        copies = [
            push(back.at[lax.rem(seat + k, size)], landed.at[seat], sems[4].at[k], sems[5].at[k],
                 peer(level, k))
            for k in range(1, size)
        ]
        landed[seat] = back[seat]
        for copy in copies:
            copy.wait()
        tiles = [landed[j] for j in range(size)]
        return (
            jnp.concatenate([t[:, :runs] for t in tiles], axis=1),
            jnp.concatenate([t[:, runs:] for t in tiles], axis=1),
        )

    incoming, later = solve(
        0, end_state[...], first_state[...], end_map[:, :width], first_map[:, :width]
    )
    result[:width] = incoming
    result[width:] = later


def border_pass(end_state, first_state, end_map, first_map):
    count = lax.axis_size("tm")
    width, runs = end_state.shape
    sizes = (2, 2, count // 4) if count % 4 == 0 and count > 4 else (count,)
    scratch = []
    piece = runs
    for size in sizes:
        piece //= size
        tiles = pltpu.VMEM((size, width, 2 * piece), f32)
        scratch += [tiles, tiles, pltpu.VMEM((size, width, 2 * width), f32), tiles, tiles]
        scratch += [pltpu.SemaphoreType.DMA((size,))] * 6
    return pl.pallas_call(
        lambda *refs: border_kernel(sizes, *refs),
        in_specs=[pl.BlockSpec(memory_space=pltpu.VMEM)] * 4,
        out_specs=pl.BlockSpec(memory_space=pltpu.VMEM),
        out_shape=jax.ShapeDtypeStruct((2 * width, runs), f32),
        scratch_shapes=scratch,
        compiler_params=pltpu.CompilerParams(
            collective_id=0, has_side_effects=True, vmem_limit_bytes=32 * 2**20
        ),
    )(end_state, first_state, end_map, first_map)


def close_kernel(per, partial, maps, carries, smoothed, parts):
    @pl.when(pl.program_id(0) == 0)
    def _():
        parts[...] = state_parts(carries[...])

    for i in range(per):
        m = maps[i]
        high = m.astype(bf16)
        low = (m - high.astype(f32)).astype(bf16)
        smoothed[i] = partial[i] + dot32(jnp.concatenate([high, low, high], axis=1), parts[...])


def close_pass(partial, maps, carries):
    steps, width, runs = partial.shape
    per = 4
    body = lambda *refs: close_kernel(per, *refs)
    along = lambda i: (i, 0, 0)
    return pl.pallas_call(
        body,
        grid=(steps // per,),
        in_specs=[
            pl.BlockSpec((per, width, runs), along),
            pl.BlockSpec((per,) + maps.shape[1:], along),
            pl.BlockSpec(carries.shape, lambda i: (0, 0)),
        ],
        out_specs=pl.BlockSpec((per, width, runs), along),
        out_shape=jax.ShapeDtypeStruct(partial.shape, f32),
        scratch_shapes=[pltpu.VMEM((3 * carries.shape[0], runs), bf16)],
        compiler_params=pltpu.CompilerParams(vmem_limit_bytes=56 * 2**20),
    )(partial, maps, carries)


def shards(
    process_noise,
    gauge_reads,
    sensor_active,
    sensor_link,
    reflectors,
    decay_rates,
    turn_angles,
    gauge_gain,
):
    steps, width, runs = process_noise.shape
    count = lax.axis_size("tm")
    rotation = rotation_basis(reflectors)
    blocks = pair_blocks(decay_rates, turn_angles)
    transition = jnp.dot(
        jnp.dot(rotation, blocks, precision=exact_mode), rotation.T, precision=exact_mode
    )
    positions = jnp.arange(width)
    onehot = (positions[None, :] == 2 * sensor_link[:, None]).astype(f32)
    active = sensor_active.astype(f32)
    counts = jnp.dot(active, onehot, precision=exact_mode)
    retain = jnp.exp(counts * jnp.log1p(-gauge_gain)[None, :])
    spread = jnp.repeat(jnp.sqrt(-jnp.expm1(-2.0 * decay_rates)), 2)
    last_row = (jnp.arange(steps) == steps - 1)[:, None]
    final_device = lax.axis_index("tm") == count - 1
    keep = jnp.where(jnp.logical_and(last_row, final_device), 0.0, retain)
    gain_high, gain_low = two_parts(gauge_gain)
    placed = (onehot.T.astype(bf16))[None] * sensor_active.astype(bf16)[:, None, :]
    weights = jnp.concatenate(
        [
            jnp.broadcast_to(rotation.astype(bf16)[None], (steps, width, width)),
            gain_high[None, :, None] * placed,
            gain_low[None, :, None] * placed,
        ],
        axis=2,
    )
    partial, maps, end_state, end_map, first_state, first_map = local_pass(
        process_noise, gauge_reads, weights, spread[:, None], retain[:, :, None],
        keep[:, :, None], map_parts(transition), map_parts(transition.T), transition,
    )
    carries = border_pass(end_state, first_state, end_map, first_map)
    return close_pass(partial, maps, carries)


def solution(mesh):
    in_specs = (
        P(("groups", "tm"), None, None),
        P(("groups", "tm"), None, None),
        P(("groups", "tm"), None),
        P(),
        P("groups", None),
        P("groups"),
        P("groups"),
        P("groups"),
    )
    out_specs = P(("groups", "tm"), None, None)
    return jax.shard_map(shards, mesh=mesh, in_specs=in_specs, out_specs=out_specs, check_vma=False)
```

```python
import jax
import jax.numpy as jnp
from jax import lax
from jax.experimental import pallas as pl
from jax.experimental.pallas import tpu as pltpu
from jax.sharding import PartitionSpec as P

exact_mode = lax.Precision.HIGHEST
bf16 = jnp.bfloat16
f32 = jnp.float32


def two_parts(x):
    high = x.astype(bf16)
    return high, (x - high.astype(f32)).astype(bf16)


def map_parts(matrix):
    high, low = two_parts(matrix)
    return jnp.concatenate([high, low, high], axis=1)


def index_of(shape):
    return lax.broadcasted_iota(jnp.int32, shape, 0), lax.broadcasted_iota(jnp.int32, shape, 1)


def as_column(line):
    row, col = index_of((line.shape[1], line.shape[1]))
    return jnp.sum(jnp.where(row == col, line, 0.0), axis=1, keepdims=True)


def pair_column(line):
    row, col = index_of((2 * line.shape[1], line.shape[1]))
    return jnp.sum(jnp.where(row // 2 == col, line, 0.0), axis=1, keepdims=True)


def across(a, b, precision=None):
    return lax.dot_general(
        a, b, (((1,), (1,)), ((), ())), precision=precision, preferred_element_type=f32
    )


def prepare(
    active, link, reflectors, decay, turn, gain, scale,
    spread, retain, fwd_map, bwd_map, trans, base, mask,
):
    steps = active.shape[0]
    width = trans.shape[0]
    row, col = index_of((width, width))
    rotation = jnp.where(row == col, 1.0, 0.0)
    for number in range(reflectors.shape[0]):
        vector = reflectors[number : number + 1, :]
        factor = 2.0 / (jnp.sum(vector * vector, axis=1, keepdims=True) + 1e-06)
        hit = jnp.sum(rotation * vector, axis=1, keepdims=True)
        rotation = rotation - factor * (hit * vector)
    decays, turns = pair_column(decay[...]), pair_column(turn[...])
    radius = jnp.exp(-decays)
    cosine, sine = radius * jnp.cos(turns), radius * jnp.sin(turns)
    element = jnp.where(row % 2 == col % 2, cosine, jnp.where(row % 2 == 0, -sine, sine))
    blocks = jnp.where(row // 2 == col // 2, element, 0.0)
    turned = jnp.dot(rotation, blocks, precision=exact_mode, preferred_element_type=f32)
    transition = across(turned, rotation, exact_mode)
    trans[...] = transition
    fwd_map[...] = map_parts(transition)
    bwd_map[...] = map_parts(transition.T)
    spread[...] = pair_column(scale[...])
    gains = as_column(gain[...])
    gauge_row, _ = index_of((width, link.shape[1]))
    placed = jnp.where(gauge_row == 2 * link[...], 1.0, 0.0)
    on = active[...].astype(f32)
    counts = across(placed.astype(bf16), on.astype(bf16))
    rates = jnp.exp(counts * jnp.log1p(-gains))
    for t in range(steps):
        retain[t] = rates[:, t : t + 1]
    high, low = two_parts(gains)
    base[...] = jnp.concatenate(
        [rotation.astype(bf16).astype(f32), high.astype(f32) * placed, low.astype(f32) * placed],
        axis=1,
    )
    mask[...] = jnp.concatenate([jnp.ones((steps, width), f32), on, on], axis=1)


def state_parts(x):
    high = x.astype(bf16)
    low = (x - high.astype(f32)).astype(bf16)
    return jnp.concatenate([high, high, low], axis=0)


def dot32(a, b):
    return jnp.dot(a, b, preferred_element_type=f32)


def local_kernel(
    blocks, per, noise, gauges, active, link, reflectors, decay, turn, gain, scale,
    partial, maps, end_state, end_map, first_state, first_map,
    filt, filt_x, pred, pred_x, run, run_x, spread, retain, fwd_map, bwd_map, trans, base, mask,
):
    step = pl.program_id(0)
    width = trans.shape[0]
    final_device = lax.axis_index("tm") == lax.axis_size("tm") - 1

    @pl.when(step == 0)
    def _():
        prepare(
            active, link, reflectors, decay, turn, gain, scale,
            spread, retain, fwd_map, bwd_map, trans, base, mask,
        )
        run[...] = jnp.zeros_like(run)
        run_x[...] = jnp.concatenate([trans[...], jnp.zeros(trans.shape, f32)], axis=1)

    @pl.when(step < blocks)
    def _():
        p, px = run[...], run_x[...]
        for i in range(per):
            t = step * per + i
            scaled = (spread[...] * noise[i].astype(f32)).astype(bf16)
            reads = gauges[i]
            weights = (base[...] * mask[pl.ds(t, 1), :]).astype(bf16)
            offset = dot32(weights, jnp.concatenate([scaled, reads, reads], axis=0))
            rate = retain[t]
            f = rate * p + offset
            fx = rate * px
            filt[t] = f
            filt_x[t] = fx
            p = dot32(fwd_map[...], state_parts(f))
            px = dot32(fwd_map[...], state_parts(fx))
            pred[t] = p
            pred_x[t] = px
        run[...] = p
        run_x[...] = px

        @pl.when(step == blocks - 1)
        def _():
            end_state[...] = f
            end_map[...] = fx
            retain[t] = jnp.where(final_device, 0.0, rate)
            run[...] = jnp.zeros_like(run)
            row = lax.broadcasted_iota(jnp.int32, run_x.shape, 0)
            col = lax.broadcasted_iota(jnp.int32, run_x.shape, 1)
            run_x[...] = jnp.where(col == row + width, 1.0, 0.0)

    @pl.when(step >= blocks)
    def _():
        s, sx = run[...], run_x[...]
        for i in reversed(range(per)):
            t = (2 * blocks - 1 - step) * per + i
            rate = retain[t]
            s = filt[t] + dot32(bwd_map[...], state_parts(rate * (s - pred[t])))
            sx = filt_x[t] + dot32(bwd_map[...], state_parts(rate * (sx - pred_x[t])))
            partial[i] = s
            maps[i] = sx
        run[...] = s
        run_x[...] = sx

        @pl.when(step == 2 * blocks - 1)
        def _():
            first_state[...] = s
            first_map[...] = sx


def local_pass(noise, gauges, *terms):
    steps, width, runs = noise.shape
    per = 4
    blocks = steps // per
    ahead = lambda i: (jnp.minimum(i, blocks - 1), 0, 0)
    back = lambda i: (jnp.minimum(2 * blocks - 1 - i, blocks - 1), 0, 0)
    whole2 = lambda i: (0, 0)
    whole3 = lambda i: (0, 0, 0)
    full = lambda x: pl.BlockSpec(x.shape, whole3 if x.ndim == 3 else whole2)
    extra = 2 * width
    body = lambda *refs: local_kernel(blocks, per, *refs)
    return pl.pallas_call(
        body,
        grid=(2 * blocks,),
        in_specs=[
            pl.BlockSpec((per,) + noise.shape[1:], ahead),
            pl.BlockSpec((per,) + gauges.shape[1:], ahead),
            *[full(x) for x in terms],
        ],
        out_specs=[
            pl.BlockSpec((per, width, runs), back),
            pl.BlockSpec((per, width, extra), back),
            pl.BlockSpec((width, runs), whole2),
            pl.BlockSpec((width, extra), whole2),
            pl.BlockSpec((width, runs), whole2),
            pl.BlockSpec((width, extra), whole2),
        ],
        out_shape=[
            jax.ShapeDtypeStruct((steps, width, runs), f32),
            jax.ShapeDtypeStruct((steps, width, extra), f32),
            jax.ShapeDtypeStruct((width, runs), f32),
            jax.ShapeDtypeStruct((width, extra), f32),
            jax.ShapeDtypeStruct((width, runs), f32),
            jax.ShapeDtypeStruct((width, extra), f32),
        ],
        scratch_shapes=[
            pltpu.VMEM((steps, width, runs), f32),
            pltpu.VMEM((steps, width, extra), f32),
            pltpu.VMEM((steps, width, runs), f32),
            pltpu.VMEM((steps, width, extra), f32),
            pltpu.VMEM((width, runs), f32),
            pltpu.VMEM((width, extra), f32),
            pltpu.VMEM((width, 1), f32),
            pltpu.VMEM((steps, width, 1), f32),
            pltpu.VMEM((width, 3 * width), bf16),
            pltpu.VMEM((width, 3 * width), bf16),
            pltpu.VMEM((width, width), f32),
            pltpu.VMEM((width, width + 2 * gauges.shape[1]), f32),
            pltpu.VMEM((steps, width + 2 * gauges.shape[1]), f32),
        ],
        compiler_params=pltpu.CompilerParams(vmem_limit_bytes=52 * 2**20),
    )(noise, gauges, *terms)


def split_dot(matrix, state):
    high = matrix.astype(bf16)
    low = (matrix - high.astype(f32)).astype(bf16)
    return dot32(jnp.concatenate([high, low, high], axis=1), state_parts(state))


def border_kernel(sizes, end_state, first_state, end_map, first_map, result, *scratch):
    me = lax.axis_index("tm")
    width = end_state.shape[0]
    last = len(sizes) - 1
    strides, seats = [], []
    stride = 1
    for size in sizes:
        strides.append(stride)
        seats.append(lax.rem(lax.div(me, stride), size))
        stride *= size

    def peer(level, k):
        seat = seats[level]
        return me + (lax.rem(seat + k, sizes[level]) - seat) * strides[level]

    barrier = pltpu.get_barrier_semaphore()
    for level, size in enumerate(sizes):
        for k in range(1, size):
            pl.semaphore_signal(
                barrier, inc=1, device_id={"tm": peer(level, k)},
                device_id_type=pl.DeviceIdType.MESH,
            )
    pl.semaphore_wait(barrier, sum(sizes) - len(sizes))

    def push(source, target, send, recv, where):
        copy = pltpu.make_async_remote_copy(
            src_ref=source, dst_ref=target, send_sem=send, recv_sem=recv,
            device_id={"tm": where}, device_id_type=pl.DeviceIdType.MESH,
        )
        copy.start()
        return copy

    def solve(level, state, first, stay, turn):
        own, got, maps, back, landed, *sems = scratch[11 * level : 11 * (level + 1)]
        size, seat = sizes[level], seats[level]
        runs = state.shape[1] // size
        top = level == last
        maps[seat] = jnp.concatenate([stay, turn], axis=1)
        for j in range(size):
            part = slice(j * runs, (j + 1) * runs)
            own[j] = jnp.concatenate([state[:, part], first[:, part]], axis=1)
        copies = []
        for k in range(1, size):
            where = peer(level, k)
            copies.append(push(maps.at[seat], maps.at[seat], sems[0].at[k], sems[1].at[k], where))
            copies.append(
                push(own.at[lax.rem(seat + k, size)], got.at[seat], sems[2].at[k], sems[3].at[k], where)
            )
        got[seat] = own[seat]
        for copy in copies:
            copy.wait()

        row = lax.broadcasted_iota(jnp.int32, (width, 2 * width), 0)
        col = lax.broadcasted_iota(jnp.int32, (width, 2 * width), 1)
        zero = jnp.zeros((width, runs), f32)
        blank = jnp.zeros((width, 2 * width), f32)

        def wide(value, extra):
            return value if top else jnp.concatenate([value, extra], axis=1)

        ahead, pulled, behind = [], [], [None] * size
        carry = wide(zero, jnp.where(row == col, 1.0, 0.0))
        for d in range(size):
            tile, both = got[d], maps[d]
            ahead.append(carry)
            pulled.append(wide(tile[:, runs:], blank) + split_dot(both[:, width:], carry))
            if not (top and d == size - 1):
                carry = wide(tile[:, :runs], blank) + split_dot(both[:, :width], carry)
        end = carry
        carry = wide(zero, jnp.where(row + width == col, 1.0, 0.0))
        for d in reversed(range(size)):
            behind[d] = carry
            if not (top and d == 0):
                carry = pulled[d] + split_dot(maps[d][:, :width].T, carry)
        if not top:
            inner = slice(runs, runs + width)
            outer = jnp.concatenate(
                solve(level + 1, end[:, :runs], carry[:, :runs], end[:, inner], carry[:, inner]),
                axis=0,
            )
        for d in range(size):
            f, s = ahead[d], behind[d]
            if not top:
                f = f[:, :runs] + split_dot(f[:, runs:], outer)
                s = s[:, :runs] + split_dot(s[:, runs:], outer)
            back[d] = jnp.concatenate([f, s], axis=1)
        copies = [
            push(back.at[lax.rem(seat + k, size)], landed.at[seat], sems[4].at[k], sems[5].at[k],
                 peer(level, k))
            for k in range(1, size)
        ]
        landed[seat] = back[seat]
        for copy in copies:
            copy.wait()
        tiles = [landed[j] for j in range(size)]
        return (
            jnp.concatenate([t[:, :runs] for t in tiles], axis=1),
            jnp.concatenate([t[:, runs:] for t in tiles], axis=1),
        )

    incoming, later = solve(
        0, end_state[...], first_state[...], end_map[:, :width], first_map[:, :width]
    )
    result[:width] = incoming
    result[width:] = later


def border_pass(end_state, first_state, end_map, first_map):
    count = lax.axis_size("tm")
    width, runs = end_state.shape
    sizes = (2, 2, count // 4) if count % 4 == 0 and count > 4 else (count,)
    scratch = []
    piece = runs
    for size in sizes:
        piece //= size
        tiles = pltpu.VMEM((size, width, 2 * piece), f32)
        scratch += [tiles, tiles, pltpu.VMEM((size, width, 2 * width), f32), tiles, tiles]
        scratch += [pltpu.SemaphoreType.DMA((size,))] * 6
    return pl.pallas_call(
        lambda *refs: border_kernel(sizes, *refs),
        in_specs=[pl.BlockSpec(memory_space=pltpu.VMEM)] * 4,
        out_specs=pl.BlockSpec(memory_space=pltpu.VMEM),
        out_shape=jax.ShapeDtypeStruct((2 * width, runs), f32),
        scratch_shapes=scratch,
        compiler_params=pltpu.CompilerParams(
            collective_id=0, has_side_effects=True, vmem_limit_bytes=32 * 2**20
        ),
    )(end_state, first_state, end_map, first_map)


def close_kernel(per, partial, maps, carries, smoothed, parts):
    @pl.when(pl.program_id(0) == 0)
    def _():
        parts[...] = state_parts(carries[...])

    for i in range(per):
        m = maps[i]
        high = m.astype(bf16)
        low = (m - high.astype(f32)).astype(bf16)
        smoothed[i] = partial[i] + dot32(jnp.concatenate([high, low, high], axis=1), parts[...])


def close_pass(partial, maps, carries):
    steps, width, runs = partial.shape
    per = 4
    body = lambda *refs: close_kernel(per, *refs)
    along = lambda i: (i, 0, 0)
    return pl.pallas_call(
        body,
        grid=(steps // per,),
        in_specs=[
            pl.BlockSpec((per, width, runs), along),
            pl.BlockSpec((per,) + maps.shape[1:], along),
            pl.BlockSpec(carries.shape, lambda i: (0, 0)),
        ],
        out_specs=pl.BlockSpec((per, width, runs), along),
        out_shape=jax.ShapeDtypeStruct(partial.shape, f32),
        scratch_shapes=[pltpu.VMEM((3 * carries.shape[0], runs), bf16)],
        compiler_params=pltpu.CompilerParams(vmem_limit_bytes=32 * 2**20),
    )(partial, maps, carries)


def shards(
    process_noise,
    gauge_reads,
    sensor_active,
    sensor_link,
    reflectors,
    decay_rates,
    turn_angles,
    gauge_gain,
):
    partial, maps, end_state, end_map, first_state, first_map = local_pass(
        process_noise, gauge_reads, sensor_active, sensor_link[None], reflectors,
        decay_rates[None], turn_angles[None], gauge_gain[None],
        jnp.sqrt(-jnp.expm1(-2.0 * decay_rates))[None],
    )
    carries = border_pass(end_state, first_state, end_map, first_map)
    return close_pass(partial, maps, carries)


def solution(mesh):
    in_specs = (
        P(("groups", "tm"), None, None),
        P(("groups", "tm"), None, None),
        P(("groups", "tm"), None),
        P(),
        P("groups", None),
        P("groups"),
        P("groups"),
        P("groups"),
    )
    out_specs = P(("groups", "tm"), None, None)
    return jax.shard_map(shards, mesh=mesh, in_specs=in_specs, out_specs=out_specs, check_vma=False)
```

```python
import jax
import jax.numpy as jnp
from jax import lax
from jax.experimental import pallas as pl
from jax.experimental.pallas import tpu as pltpu
from jax.sharding import PartitionSpec as P

exact_mode = lax.Precision.HIGHEST
bf16 = jnp.bfloat16
f32 = jnp.float32


def two_parts(x):
    high = x.astype(bf16)
    return high, (x - high.astype(f32)).astype(bf16)


def map_parts(matrix):
    high, low = two_parts(matrix)
    return jnp.concatenate([high, low, high], axis=1)


def index_of(shape):
    return lax.broadcasted_iota(jnp.int32, shape, 0), lax.broadcasted_iota(jnp.int32, shape, 1)


def as_column(line):
    row, col = index_of((line.shape[1], line.shape[1]))
    return jnp.sum(jnp.where(row == col, line, 0.0), axis=1, keepdims=True)


def pair_column(line):
    row, col = index_of((2 * line.shape[1], line.shape[1]))
    return jnp.sum(jnp.where(row // 2 == col, line, 0.0), axis=1, keepdims=True)


def across(a, b, precision=None):
    return lax.dot_general(
        a, b, (((1,), (1,)), ((), ())), precision=precision, preferred_element_type=f32
    )


def prepare(
    active, link, reflectors, decay, turn, gain, scale,
    spread, retain, fwd_map, bwd_map, trans, base, mask,
):
    steps = active.shape[0]
    width = trans.shape[0]
    row, col = index_of((width, width))
    rotation = jnp.where(row == col, 1.0, 0.0)
    for number in range(reflectors.shape[0]):
        vector = reflectors[number : number + 1, :]
        factor = 2.0 / (jnp.sum(vector * vector, axis=1, keepdims=True) + 1e-06)
        hit = jnp.sum(rotation * vector, axis=1, keepdims=True)
        rotation = rotation - factor * (hit * vector)
    decays, turns = pair_column(decay[...]), pair_column(turn[...])
    radius = jnp.exp(-decays)
    cosine, sine = radius * jnp.cos(turns), radius * jnp.sin(turns)
    element = jnp.where(row % 2 == col % 2, cosine, jnp.where(row % 2 == 0, -sine, sine))
    blocks = jnp.where(row // 2 == col // 2, element, 0.0)
    turned = jnp.dot(rotation, blocks, precision=exact_mode, preferred_element_type=f32)
    transition = across(turned, rotation, exact_mode)
    trans[...] = transition
    fwd_map[...] = map_parts(transition)
    bwd_map[...] = map_parts(transition.T)
    spread[...] = pair_column(scale[...])
    gains = as_column(gain[...])
    gauge_row, _ = index_of((width, link.shape[1]))
    placed = jnp.where(gauge_row == 2 * link[...], 1.0, 0.0)
    on = active[...].astype(f32)
    counts = across(placed.astype(bf16), on.astype(bf16))
    rates = jnp.exp(counts * jnp.log1p(-gains))
    for t in range(steps):
        retain[t] = rates[:, t : t + 1]
    high, low = two_parts(gains)
    base[...] = jnp.concatenate(
        [rotation.astype(bf16).astype(f32), high.astype(f32) * placed, low.astype(f32) * placed],
        axis=1,
    )
    mask[...] = jnp.concatenate([jnp.ones((steps, width), f32), on, on], axis=1)


def state_parts(x):
    high = x.astype(bf16)
    low = (x - high.astype(f32)).astype(bf16)
    return jnp.concatenate([high, high, low], axis=0)


def dot32(a, b):
    return jnp.dot(a, b, preferred_element_type=f32)


def local_kernel(
    blocks, per, noise, gauges, active, link, reflectors, decay, turn, gain, scale,
    partial, maps, end_state, end_map, first_state, first_map,
    filt, filt_x, pred, pred_x, run, run_x, spread, retain, fwd_map, bwd_map, trans, base, mask,
):
    step = pl.program_id(0)
    width = trans.shape[0]
    final_device = lax.axis_index("tm") == lax.axis_size("tm") - 1

    @pl.when(step == 0)
    def _():
        prepare(
            active, link, reflectors, decay, turn, gain, scale,
            spread, retain, fwd_map, bwd_map, trans, base, mask,
        )
        run[...] = jnp.zeros_like(run)
        run_x[...] = jnp.concatenate([trans[...], jnp.zeros(trans.shape, f32)], axis=1)

    @pl.when(step < blocks)
    def _():
        p, px = run[...], run_x[...]
        for i in range(per):
            t = step * per + i
            scaled = (spread[...] * noise[i].astype(f32)).astype(bf16)
            reads = gauges[i]
            weights = (base[...] * mask[pl.ds(t, 1), :]).astype(bf16)
            offset = dot32(weights, jnp.concatenate([scaled, reads, reads], axis=0))
            rate = retain[t]
            f = rate * p + offset
            fx = rate * px
            filt[t] = f
            filt_x[t] = fx
            p = dot32(fwd_map[...], state_parts(f))
            px = dot32(fwd_map[...], state_parts(fx))
            pred[t] = p
            pred_x[t] = px
        run[...] = p
        run_x[...] = px

        @pl.when(step == blocks - 1)
        def _():
            end_state[...] = f
            end_map[...] = fx
            retain[t] = jnp.where(final_device, 0.0, rate)
            run[...] = jnp.zeros_like(run)
            row = lax.broadcasted_iota(jnp.int32, run_x.shape, 0)
            col = lax.broadcasted_iota(jnp.int32, run_x.shape, 1)
            run_x[...] = jnp.where(col == row + width, 1.0, 0.0)

    @pl.when(step >= blocks)
    def _():
        s, sx = run[...], run_x[...]
        for i in reversed(range(per)):
            t = (2 * blocks - 1 - step) * per + i
            rate = retain[t]
            s = filt[t] + dot32(bwd_map[...], state_parts(rate * (s - pred[t])))
            sx = filt_x[t] + dot32(bwd_map[...], state_parts(rate * (sx - pred_x[t])))
            partial[i] = s.astype(bf16)
            maps[i] = sx
        run[...] = s
        run_x[...] = sx

        @pl.when(step == 2 * blocks - 1)
        def _():
            first_state[...] = s
            first_map[...] = sx


def local_pass(noise, gauges, *terms):
    steps, width, runs = noise.shape
    per = 4
    blocks = steps // per
    ahead = lambda i: (jnp.minimum(i, blocks - 1), 0, 0)
    back = lambda i: (jnp.minimum(2 * blocks - 1 - i, blocks - 1), 0, 0)
    whole2 = lambda i: (0, 0)
    whole3 = lambda i: (0, 0, 0)
    full = lambda x: pl.BlockSpec(x.shape, whole3 if x.ndim == 3 else whole2)
    extra = 2 * width
    body = lambda *refs: local_kernel(blocks, per, *refs)
    return pl.pallas_call(
        body,
        grid=(2 * blocks,),
        in_specs=[
            pl.BlockSpec((per,) + noise.shape[1:], ahead),
            pl.BlockSpec((per,) + gauges.shape[1:], ahead),
            *[full(x) for x in terms],
        ],
        out_specs=[
            pl.BlockSpec((per, width, runs), back),
            pl.BlockSpec((per, width, extra), back),
            pl.BlockSpec((width, runs), whole2),
            pl.BlockSpec((width, extra), whole2),
            pl.BlockSpec((width, runs), whole2),
            pl.BlockSpec((width, extra), whole2),
        ],
        out_shape=[
            jax.ShapeDtypeStruct((steps, width, runs), bf16),
            jax.ShapeDtypeStruct((steps, width, extra), f32),
            jax.ShapeDtypeStruct((width, runs), f32),
            jax.ShapeDtypeStruct((width, extra), f32),
            jax.ShapeDtypeStruct((width, runs), f32),
            jax.ShapeDtypeStruct((width, extra), f32),
        ],
        scratch_shapes=[
            pltpu.VMEM((steps, width, runs), f32),
            pltpu.VMEM((steps, width, extra), f32),
            pltpu.VMEM((steps, width, runs), f32),
            pltpu.VMEM((steps, width, extra), f32),
            pltpu.VMEM((width, runs), f32),
            pltpu.VMEM((width, extra), f32),
            pltpu.VMEM((width, 1), f32),
            pltpu.VMEM((steps, width, 1), f32),
            pltpu.VMEM((width, 3 * width), bf16),
            pltpu.VMEM((width, 3 * width), bf16),
            pltpu.VMEM((width, width), f32),
            pltpu.VMEM((width, width + 2 * gauges.shape[1]), f32),
            pltpu.VMEM((steps, width + 2 * gauges.shape[1]), f32),
        ],
        compiler_params=pltpu.CompilerParams(vmem_limit_bytes=62 * 2**20),
    )(noise, gauges, *terms)


def split_dot(matrix, state):
    high = matrix.astype(bf16)
    low = (matrix - high.astype(f32)).astype(bf16)
    return dot32(jnp.concatenate([high, low, high], axis=1), state_parts(state))


def border_kernel(sizes, end_state, first_state, end_map, first_map, result, *scratch):
    me = lax.axis_index("tm")
    width = end_state.shape[0]
    last = len(sizes) - 1
    strides, seats = [], []
    stride = 1
    for size in sizes:
        strides.append(stride)
        seats.append(lax.rem(lax.div(me, stride), size))
        stride *= size

    def peer(level, k):
        seat = seats[level]
        return me + (lax.rem(seat + k, sizes[level]) - seat) * strides[level]

    barrier = pltpu.get_barrier_semaphore()
    for level, size in enumerate(sizes):
        for k in range(1, size):
            pl.semaphore_signal(
                barrier, inc=1, device_id={"tm": peer(level, k)},
                device_id_type=pl.DeviceIdType.MESH,
            )
    pl.semaphore_wait(barrier, sum(sizes) - len(sizes))

    def push(source, target, send, recv, where):
        copy = pltpu.make_async_remote_copy(
            src_ref=source, dst_ref=target, send_sem=send, recv_sem=recv,
            device_id={"tm": where}, device_id_type=pl.DeviceIdType.MESH,
        )
        copy.start()
        return copy

    def solve(level, state, first, stay, turn):
        own, got, maps, back, landed, *sems = scratch[11 * level : 11 * (level + 1)]
        size, seat = sizes[level], seats[level]
        runs = state.shape[1] // size
        top = level == last
        maps[seat] = jnp.concatenate([stay, turn], axis=1)
        for j in range(size):
            part = slice(j * runs, (j + 1) * runs)
            own[j] = jnp.concatenate([state[:, part], first[:, part]], axis=1)
        copies = []
        for k in range(1, size):
            where = peer(level, k)
            copies.append(push(maps.at[seat], maps.at[seat], sems[0].at[k], sems[1].at[k], where))
            copies.append(
                push(own.at[lax.rem(seat + k, size)], got.at[seat], sems[2].at[k], sems[3].at[k], where)
            )
        got[seat] = own[seat]
        for copy in copies:
            copy.wait()

        row = lax.broadcasted_iota(jnp.int32, (width, 2 * width), 0)
        col = lax.broadcasted_iota(jnp.int32, (width, 2 * width), 1)
        zero = jnp.zeros((width, runs), f32)
        blank = jnp.zeros((width, 2 * width), f32)

        def wide(value, extra):
            return value if top else jnp.concatenate([value, extra], axis=1)

        ahead, pulled, behind = [], [], [None] * size
        carry = wide(zero, jnp.where(row == col, 1.0, 0.0))
        for d in range(size):
            tile, both = got[d], maps[d]
            ahead.append(carry)
            pulled.append(wide(tile[:, runs:], blank) + split_dot(both[:, width:], carry))
            if not (top and d == size - 1):
                carry = wide(tile[:, :runs], blank) + split_dot(both[:, :width], carry)
        end = carry
        carry = wide(zero, jnp.where(row + width == col, 1.0, 0.0))
        for d in reversed(range(size)):
            behind[d] = carry
            if not (top and d == 0):
                carry = pulled[d] + split_dot(maps[d][:, :width].T, carry)
        if not top:
            inner = slice(runs, runs + width)
            outer = jnp.concatenate(
                solve(level + 1, end[:, :runs], carry[:, :runs], end[:, inner], carry[:, inner]),
                axis=0,
            )
        for d in range(size):
            f, s = ahead[d], behind[d]
            if not top:
                f = f[:, :runs] + split_dot(f[:, runs:], outer)
                s = s[:, :runs] + split_dot(s[:, runs:], outer)
            back[d] = jnp.concatenate([f, s], axis=1)
        copies = [
            push(back.at[lax.rem(seat + k, size)], landed.at[seat], sems[4].at[k], sems[5].at[k],
                 peer(level, k))
            for k in range(1, size)
        ]
        landed[seat] = back[seat]
        for copy in copies:
            copy.wait()
        tiles = [landed[j] for j in range(size)]
        return (
            jnp.concatenate([t[:, :runs] for t in tiles], axis=1),
            jnp.concatenate([t[:, runs:] for t in tiles], axis=1),
        )

    incoming, later = solve(
        0, end_state[...], first_state[...], end_map[:, :width], first_map[:, :width]
    )
    result[:width] = incoming
    result[width:] = later


def border_pass(end_state, first_state, end_map, first_map):
    count = lax.axis_size("tm")
    width, runs = end_state.shape
    sizes = (2, 2, count // 4) if count % 4 == 0 and count > 4 else (count,)
    scratch = []
    piece = runs
    for size in sizes:
        piece //= size
        tiles = pltpu.VMEM((size, width, 2 * piece), f32)
        scratch += [tiles, tiles, pltpu.VMEM((size, width, 2 * width), f32), tiles, tiles]
        scratch += [pltpu.SemaphoreType.DMA((size,))] * 6
    return pl.pallas_call(
        lambda *refs: border_kernel(sizes, *refs),
        in_specs=[pl.BlockSpec(memory_space=pltpu.VMEM)] * 4,
        out_specs=pl.BlockSpec(memory_space=pltpu.VMEM),
        out_shape=jax.ShapeDtypeStruct((2 * width, runs), f32),
        scratch_shapes=scratch,
        compiler_params=pltpu.CompilerParams(
            collective_id=0, has_side_effects=True, vmem_limit_bytes=32 * 2**20
        ),
    )(end_state, first_state, end_map, first_map)


def close_kernel(per, partial, maps, carries, smoothed, parts):
    @pl.when(pl.program_id(0) == 0)
    def _():
        parts[...] = state_parts(carries[...])

    for i in range(per):
        m = maps[i]
        high = m.astype(bf16)
        low = (m - high.astype(f32)).astype(bf16)
        smoothed[i] = partial[i].astype(f32) + dot32(jnp.concatenate([high, low, high], axis=1), parts[...])


def close_pass(partial, maps, carries):
    steps, width, runs = partial.shape
    per = 4
    body = lambda *refs: close_kernel(per, *refs)
    along = lambda i: (i, 0, 0)
    return pl.pallas_call(
        body,
        grid=(steps // per,),
        in_specs=[
            pl.BlockSpec((per, width, runs), along),
            pl.BlockSpec((per,) + maps.shape[1:], along),
            pl.BlockSpec(carries.shape, lambda i: (0, 0)),
        ],
        out_specs=pl.BlockSpec((per, width, runs), along),
        out_shape=jax.ShapeDtypeStruct(partial.shape, f32),
        scratch_shapes=[pltpu.VMEM((3 * carries.shape[0], runs), bf16)],
        compiler_params=pltpu.CompilerParams(vmem_limit_bytes=32 * 2**20),
    )(partial, maps, carries)


def shards(
    process_noise,
    gauge_reads,
    sensor_active,
    sensor_link,
    reflectors,
    decay_rates,
    turn_angles,
    gauge_gain,
):
    partial, maps, end_state, end_map, first_state, first_map = local_pass(
        process_noise, gauge_reads, sensor_active, sensor_link[None], reflectors,
        decay_rates[None], turn_angles[None], gauge_gain[None],
        jnp.sqrt(-jnp.expm1(-2.0 * decay_rates))[None],
    )
    carries = border_pass(end_state, first_state, end_map, first_map)
    return close_pass(partial, maps, carries)


def solution(mesh):
    in_specs = (
        P(("groups", "tm"), None, None),
        P(("groups", "tm"), None, None),
        P(("groups", "tm"), None),
        P(),
        P("groups", None),
        P("groups"),
        P("groups"),
        P("groups"),
    )
    out_specs = P(("groups", "tm"), None, None)
    return jax.shard_map(shards, mesh=mesh, in_specs=in_specs, out_specs=out_specs, check_vma=False)
```

```python
import jax
import jax.numpy as jnp
from jax import lax
from jax.experimental import pallas as pl
from jax.experimental.pallas import tpu as pltpu
from jax.sharding import PartitionSpec as P

exact_mode = lax.Precision.HIGHEST
bf16 = jnp.bfloat16
f32 = jnp.float32


def two_parts(x):
    high = x.astype(bf16)
    return high, (x - high.astype(f32)).astype(bf16)


def map_parts(matrix):
    high, low = two_parts(matrix)
    return jnp.concatenate([high, low, high], axis=1)


def index_of(shape):
    return lax.broadcasted_iota(jnp.int32, shape, 0), lax.broadcasted_iota(jnp.int32, shape, 1)


def as_column(line):
    row, col = index_of((line.shape[1], line.shape[1]))
    return jnp.sum(jnp.where(row == col, line, 0.0), axis=1, keepdims=True)


def pair_column(line):
    row, col = index_of((2 * line.shape[1], line.shape[1]))
    return jnp.sum(jnp.where(row // 2 == col, line, 0.0), axis=1, keepdims=True)


def across(a, b, precision=None):
    return lax.dot_general(
        a, b, (((1,), (1,)), ((), ())), precision=precision, preferred_element_type=f32
    )


def prepare(
    active, link, reflectors, decay, turn, gain, scale,
    spread, retain, fwd_map, bwd_map, trans, base, mask,
):
    steps = active.shape[0]
    width = trans.shape[0]
    row, col = index_of((width, width))
    rotation = jnp.where(row == col, 1.0, 0.0)
    for number in range(reflectors.shape[0]):
        vector = reflectors[number : number + 1, :]
        factor = 2.0 / (jnp.sum(vector * vector, axis=1, keepdims=True) + 1e-06)
        hit = jnp.sum(rotation * vector, axis=1, keepdims=True)
        rotation = rotation - factor * (hit * vector)
    decays, turns = pair_column(decay[...]), pair_column(turn[...])
    radius = jnp.exp(-decays)
    cosine, sine = radius * jnp.cos(turns), radius * jnp.sin(turns)
    element = jnp.where(row % 2 == col % 2, cosine, jnp.where(row % 2 == 0, -sine, sine))
    blocks = jnp.where(row // 2 == col // 2, element, 0.0)
    turned = jnp.dot(rotation, blocks, precision=exact_mode, preferred_element_type=f32)
    transition = across(turned, rotation, exact_mode)
    trans[...] = transition
    fwd_map[...] = map_parts(transition)
    bwd_map[...] = map_parts(transition.T)
    spread[...] = pair_column(scale[...])
    gains = as_column(gain[...])
    gauge_row, _ = index_of((width, link.shape[1]))
    placed = jnp.where(gauge_row == 2 * link[...], 1.0, 0.0)
    on = active[...].astype(f32)
    counts = across(placed.astype(bf16), on.astype(bf16))
    rates = jnp.exp(counts * jnp.log1p(-gains))
    for t in range(steps):
        retain[t] = rates[:, t : t + 1]
    high, low = two_parts(gains)
    base[...] = jnp.concatenate(
        [rotation.astype(bf16).astype(f32), high.astype(f32) * placed, low.astype(f32) * placed],
        axis=1,
    )
    mask[...] = jnp.concatenate([jnp.ones((steps, width), f32), on, on], axis=1)


def state_parts(x):
    high = x.astype(bf16)
    low = (x - high.astype(f32)).astype(bf16)
    return jnp.concatenate([high, high, low], axis=0)


def dot32(a, b):
    return jnp.dot(a, b, preferred_element_type=f32)


def local_kernel(
    blocks, per, noise, gauges, active, link, reflectors, lines,
    partial, maps, end_state, end_map, first_state, first_map,
    filt, filt_x, pred, pred_x, run, run_x, spread, retain, fwd_map, bwd_map, trans, base, mask,
):
    step = pl.program_id(0)
    width = trans.shape[0]
    final_device = lax.axis_index("tm") == lax.axis_size("tm") - 1

    @pl.when(step == 0)
    def _():
        half = width // 2
        decay, turn, scale = (lines[j : j + 1, :half] for j in range(3))
        gain = lines[3:4, :]
        prepare(
            active, link, reflectors, decay, turn, gain, scale,
            spread, retain, fwd_map, bwd_map, trans, base, mask,
        )
        run[...] = jnp.zeros_like(run)
        run_x[...] = jnp.concatenate([trans[...], jnp.zeros(trans.shape, f32)], axis=1)

    @pl.when(step < blocks)
    def _():
        p, px = run[...], run_x[...]
        for i in range(per):
            t = step * per + i
            scaled = (spread[...] * noise[i].astype(f32)).astype(bf16)
            reads = gauges[i]
            weights = (base[...] * mask[pl.ds(t, 1), :]).astype(bf16)
            offset = dot32(weights, jnp.concatenate([scaled, reads, reads], axis=0))
            rate = retain[t]
            f = rate * p + offset
            fx = rate * px
            filt[t] = f
            filt_x[t] = fx
            p = dot32(fwd_map[...], state_parts(f))
            px = dot32(fwd_map[...], state_parts(fx))
            pred[t] = p
            pred_x[t] = px
        run[...] = p
        run_x[...] = px

        @pl.when(step == blocks - 1)
        def _():
            end_state[...] = f
            end_map[...] = fx
            retain[t] = jnp.where(final_device, 0.0, rate)
            run[...] = jnp.zeros_like(run)
            row = lax.broadcasted_iota(jnp.int32, run_x.shape, 0)
            col = lax.broadcasted_iota(jnp.int32, run_x.shape, 1)
            run_x[...] = jnp.where(col == row + width, 1.0, 0.0)

    @pl.when(step >= blocks)
    def _():
        s, sx = run[...], run_x[...]
        for i in reversed(range(per)):
            t = (2 * blocks - 1 - step) * per + i
            rate = retain[t]
            s = filt[t] + dot32(bwd_map[...], state_parts(rate * (s - pred[t])))
            sx = filt_x[t] + dot32(bwd_map[...], state_parts(rate * (sx - pred_x[t])))
            partial[i] = s.astype(bf16)
            maps[i] = sx
        run[...] = s
        run_x[...] = sx

        @pl.when(step == 2 * blocks - 1)
        def _():
            first_state[...] = s
            first_map[...] = sx


def local_pass(noise, gauges, *terms):
    steps, width, runs = noise.shape
    per = 4
    blocks = steps // per
    ahead = lambda i: (jnp.minimum(i, blocks - 1), 0, 0)
    back = lambda i: (jnp.minimum(2 * blocks - 1 - i, blocks - 1), 0, 0)
    whole2 = lambda i: (0, 0)
    whole3 = lambda i: (0, 0, 0)
    full = lambda x: pl.BlockSpec(x.shape, whole3 if x.ndim == 3 else whole2)
    extra = 2 * width
    body = lambda *refs: local_kernel(blocks, per, *refs)
    return pl.pallas_call(
        body,
        grid=(2 * blocks,),
        in_specs=[
            pl.BlockSpec((per,) + noise.shape[1:], ahead),
            pl.BlockSpec((per,) + gauges.shape[1:], ahead),
            *[full(x) for x in terms],
        ],
        out_specs=[
            pl.BlockSpec((per, width, runs), back),
            pl.BlockSpec((per, width, extra), back),
            pl.BlockSpec((width, runs), whole2),
            pl.BlockSpec((width, extra), whole2),
            pl.BlockSpec((width, runs), whole2),
            pl.BlockSpec((width, extra), whole2),
        ],
        out_shape=[
            jax.ShapeDtypeStruct((steps, width, runs), bf16),
            jax.ShapeDtypeStruct((steps, width, extra), f32),
            jax.ShapeDtypeStruct((width, runs), f32),
            jax.ShapeDtypeStruct((width, extra), f32),
            jax.ShapeDtypeStruct((width, runs), f32),
            jax.ShapeDtypeStruct((width, extra), f32),
        ],
        scratch_shapes=[
            pltpu.VMEM((steps, width, runs), f32),
            pltpu.VMEM((steps, width, extra), f32),
            pltpu.VMEM((steps, width, runs), f32),
            pltpu.VMEM((steps, width, extra), f32),
            pltpu.VMEM((width, runs), f32),
            pltpu.VMEM((width, extra), f32),
            pltpu.VMEM((width, 1), f32),
            pltpu.VMEM((steps, width, 1), f32),
            pltpu.VMEM((width, 3 * width), bf16),
            pltpu.VMEM((width, 3 * width), bf16),
            pltpu.VMEM((width, width), f32),
            pltpu.VMEM((width, width + 2 * gauges.shape[1]), f32),
            pltpu.VMEM((steps, width + 2 * gauges.shape[1]), f32),
        ],
        compiler_params=pltpu.CompilerParams(vmem_limit_bytes=52 * 2**20),
    )(noise, gauges, *terms)


def split_dot(matrix, state):
    high = matrix.astype(bf16)
    low = (matrix - high.astype(f32)).astype(bf16)
    return dot32(jnp.concatenate([high, low, high], axis=1), state_parts(state))


def border_kernel(sizes, end_state, first_state, end_map, first_map, result, *scratch):
    me = lax.axis_index("tm")
    width = end_state.shape[0]
    last = len(sizes) - 1
    strides, seats = [], []
    stride = 1
    for size in sizes:
        strides.append(stride)
        seats.append(lax.rem(lax.div(me, stride), size))
        stride *= size

    def peer(level, k):
        seat = seats[level]
        return me + (lax.rem(seat + k, sizes[level]) - seat) * strides[level]

    barrier = pltpu.get_barrier_semaphore()
    for level, size in enumerate(sizes):
        for k in range(1, size):
            pl.semaphore_signal(
                barrier, inc=1, device_id={"tm": peer(level, k)},
                device_id_type=pl.DeviceIdType.MESH,
            )
    pl.semaphore_wait(barrier, sum(sizes) - len(sizes))

    def push(source, target, send, recv, where):
        copy = pltpu.make_async_remote_copy(
            src_ref=source, dst_ref=target, send_sem=send, recv_sem=recv,
            device_id={"tm": where}, device_id_type=pl.DeviceIdType.MESH,
        )
        copy.start()
        return copy

    def solve(level, state, first, stay, turn):
        own, got, maps, back, landed, *sems = scratch[11 * level : 11 * (level + 1)]
        size, seat = sizes[level], seats[level]
        runs = state.shape[1] // size
        top = level == last
        maps[seat] = jnp.concatenate([stay, turn], axis=1)
        for j in range(size):
            part = slice(j * runs, (j + 1) * runs)
            own[j] = jnp.concatenate([state[:, part], first[:, part]], axis=1)
        copies = []
        for k in range(1, size):
            where = peer(level, k)
            copies.append(push(maps.at[seat], maps.at[seat], sems[0].at[k], sems[1].at[k], where))
            copies.append(
                push(own.at[lax.rem(seat + k, size)], got.at[seat], sems[2].at[k], sems[3].at[k], where)
            )
        got[seat] = own[seat]
        for copy in copies:
            copy.wait()

        row = lax.broadcasted_iota(jnp.int32, (width, 2 * width), 0)
        col = lax.broadcasted_iota(jnp.int32, (width, 2 * width), 1)
        zero = jnp.zeros((width, runs), f32)
        blank = jnp.zeros((width, 2 * width), f32)

        def wide(value, extra):
            return value if top else jnp.concatenate([value, extra], axis=1)

        ahead, pulled, behind = [], [], [None] * size
        carry = wide(zero, jnp.where(row == col, 1.0, 0.0))
        for d in range(size):
            tile, both = got[d], maps[d]
            ahead.append(carry)
            pulled.append(wide(tile[:, runs:], blank) + split_dot(both[:, width:], carry))
            if not (top and d == size - 1):
                carry = wide(tile[:, :runs], blank) + split_dot(both[:, :width], carry)
        end = carry
        carry = wide(zero, jnp.where(row + width == col, 1.0, 0.0))
        for d in reversed(range(size)):
            behind[d] = carry
            if not (top and d == 0):
                carry = pulled[d] + split_dot(maps[d][:, :width].T, carry)
        if not top:
            inner = slice(runs, runs + width)
            outer = jnp.concatenate(
                solve(level + 1, end[:, :runs], carry[:, :runs], end[:, inner], carry[:, inner]),
                axis=0,
            )
        for d in range(size):
            f, s = ahead[d], behind[d]
            if not top:
                f = f[:, :runs] + split_dot(f[:, runs:], outer)
                s = s[:, :runs] + split_dot(s[:, runs:], outer)
            back[d] = jnp.concatenate([f, s], axis=1)
        copies = [
            push(back.at[lax.rem(seat + k, size)], landed.at[seat], sems[4].at[k], sems[5].at[k],
                 peer(level, k))
            for k in range(1, size)
        ]
        landed[seat] = back[seat]
        for copy in copies:
            copy.wait()
        tiles = [landed[j] for j in range(size)]
        return (
            jnp.concatenate([t[:, :runs] for t in tiles], axis=1),
            jnp.concatenate([t[:, runs:] for t in tiles], axis=1),
        )

    incoming, later = solve(
        0, end_state[...], first_state[...], end_map[:, :width], first_map[:, :width]
    )
    result[:width] = incoming
    result[width:] = later


def border_pass(end_state, first_state, end_map, first_map):
    count = lax.axis_size("tm")
    width, runs = end_state.shape
    sizes = (2, 2, count // 4) if count % 4 == 0 and count > 4 else (count,)
    scratch = []
    piece = runs
    for size in sizes:
        piece //= size
        tiles = pltpu.VMEM((size, width, 2 * piece), f32)
        scratch += [tiles, tiles, pltpu.VMEM((size, width, 2 * width), f32), tiles, tiles]
        scratch += [pltpu.SemaphoreType.DMA((size,))] * 6
    return pl.pallas_call(
        lambda *refs: border_kernel(sizes, *refs),
        in_specs=[pl.BlockSpec(memory_space=pltpu.VMEM)] * 4,
        out_specs=pl.BlockSpec(memory_space=pltpu.VMEM),
        out_shape=jax.ShapeDtypeStruct((2 * width, runs), f32),
        scratch_shapes=scratch,
        compiler_params=pltpu.CompilerParams(
            collective_id=0, has_side_effects=True, vmem_limit_bytes=32 * 2**20
        ),
    )(end_state, first_state, end_map, first_map)


def close_kernel(per, partial, maps, carries, smoothed, parts):
    @pl.when(pl.program_id(0) == 0)
    def _():
        parts[...] = state_parts(carries[...])

    for i in range(per):
        m = maps[i]
        high = m.astype(bf16)
        low = (m - high.astype(f32)).astype(bf16)
        smoothed[i] = partial[i].astype(f32) + dot32(jnp.concatenate([high, low, high], axis=1), parts[...])


def close_pass(partial, maps, carries):
    steps, width, runs = partial.shape
    per = 4
    body = lambda *refs: close_kernel(per, *refs)
    along = lambda i: (i, 0, 0)
    return pl.pallas_call(
        body,
        grid=(steps // per,),
        in_specs=[
            pl.BlockSpec((per, width, runs), along),
            pl.BlockSpec((per,) + maps.shape[1:], along),
            pl.BlockSpec(carries.shape, lambda i: (0, 0)),
        ],
        out_specs=pl.BlockSpec((per, width, runs), along),
        out_shape=jax.ShapeDtypeStruct(partial.shape, f32),
        scratch_shapes=[pltpu.VMEM((3 * carries.shape[0], runs), bf16)],
        compiler_params=pltpu.CompilerParams(vmem_limit_bytes=32 * 2**20),
    )(partial, maps, carries)


def shards(
    process_noise,
    gauge_reads,
    sensor_active,
    sensor_link,
    reflectors,
    decay_rates,
    turn_angles,
    gauge_gain,
):
    scale = jnp.sqrt(-jnp.expm1(-2.0 * decay_rates))
    wide = jnp.tile(jnp.stack([decay_rates, turn_angles, scale]), (1, 2))
    partial, maps, end_state, end_map, first_state, first_map = local_pass(
        process_noise, gauge_reads, sensor_active, sensor_link[None], reflectors,
        jnp.concatenate([wide, gauge_gain[None]], axis=0),
    )
    carries = border_pass(end_state, first_state, end_map, first_map)
    return close_pass(partial, maps, carries)


def solution(mesh):
    in_specs = (
        P(("groups", "tm"), None, None),
        P(("groups", "tm"), None, None),
        P(("groups", "tm"), None),
        P(),
        P("groups", None),
        P("groups"),
        P("groups"),
        P("groups"),
    )
    out_specs = P(("groups", "tm"), None, None)
    return jax.shard_map(shards, mesh=mesh, in_specs=in_specs, out_specs=out_specs, check_vma=False)
```
